32 devices in a mesh: grp: 4 (over y, core), seq: 8 (over z, x).
Axes of the slice: x: 2, y: 2, z: 4, core: 2. Of those that a mesh axis runs over, the one named last changes fastest.
Arguments:
- queries: bfloat16 [16384, 1024], P(('grp', 'seq')), may hold values from -200 to 200
- keys: bfloat16 [16384, 1024], P(('grp', 'seq')), may hold values from -5 to 5
- values: bfloat16 [16384, 1024], P(('grp', 'seq')), may hold values from -6 to 6
- out_grad: bfloat16 [16384, 1024], P(('grp', 'seq')), may hold values from -6 to 6
Outputs:
- attended: bfloat16 [16384, 1024], P(('grp', 'seq'))
- grad_queries: bfloat16 [16384, 1024], P(('grp', 'seq'))
- grad_keys: bfloat16 [16384, 1024], P(('grp', 'seq'))
- grad_values: bfloat16 [16384, 1024], P(('grp', 'seq'))
The draws below stay inside these ranges and needn't reach their ends.
All inputs are finite; a program needn't handle non-finite values.
Results may differ from the reference program's by a relative error of at most 0.02.
Values may be sent and summed in bfloat16 or wider, within the bound.
A program may use at most 128 MiB of HBM per device.

```python
import math
import jax
import jax.numpy as jnp
from jax import lax

D = 1024
H = 16
HD = 64
BLOCK = 512
P1 = 4
P2 = 32
RATIO = 8
FR_DEV = 512
FRAMES = 16384
NEAR = 128
GROUP_ROWS = 128
TOP_ROWS = 64
KEYS = 960
N_SEQ = 8


def shared_base(key):
    base_rows = jnp.clip(jax.random.normal(key, (FRAMES, D), jnp.float32), -5.0, 5.0)
    return base_rows


def draw_keys(key, part):
    base_rows = shared_base(key)
    return base_rows.astype(jnp.bfloat16)


def draw_queries(key, part):
    key = jax.random.fold_in(key, 2)
    return jnp.clip(jax.random.normal(key, (FRAMES, D), jnp.float32), -5.0, 5.0).astype(jnp.bfloat16)


def block_levels(key, extent, cuts, smallest, high):
    loudness, own = 1.0, jax.random.fold_in(key, 6)
    for dim, shards_of in cuts:
        heights = jnp.exp(jax.random.uniform(jax.random.fold_in(own, dim), (shards_of,), jnp.float32, smallest / len(cuts), high / len(cuts)))
        loudness = loudness * jnp.repeat(heights, extent[dim] // shards_of).reshape([-1 if axis == dim else 1 for axis in range(len(extent))])
    return loudness


def normal_values(own_key, shape, width, most, shards=(), kind=jnp.bfloat16):
    values = width * jax.random.normal(own_key, shape, jnp.float32)
    if shards:
        values = values * block_levels(own_key, shape, shards, -0.22, 0.18)
    return jnp.clip(values, -most, most).astype(kind)


def setup_inputs(seed: int = 0) -> dict:
    seeds = jax.random.split(jax.random.key(seed), 5)
    queries = draw_queries(jax.random.fold_in(seeds[4], 71), 0)
    keys = draw_keys(jax.random.fold_in(seeds[4], 71), 0)
    values = normal_values(seeds[2], (FRAMES, D), 1.0, 6.0, ((0, 32),))
    out_grad = normal_values(seeds[3], (FRAMES, D), 1.0, 6.0, ((0, 32),))
    return {"queries": queries, "keys": keys, "values": values, "out_grad": out_grad}


EPS = 1e-06
NEG = -1e+30
HIGH = lax.Precision.HIGHEST

def keep_bf16(value):
    rounded = lax.optimization_barrier(value.astype(jnp.bfloat16)).astype(jnp.float32)
    return value + lax.stop_gradient(rounded - value)

def summarize(stacked, factor):
    count_rows = stacked.shape[1] // factor
    pooled = lax.optimization_barrier(jnp.mean(stacked.reshape(2, count_rows, factor, H, HD), axis=2))
    scaled = pooled * lax.rsqrt(lax.optimization_barrier(jnp.mean(pooled * pooled, axis=-1, keepdims=True)) + EPS)
    return keep_bf16(scaled.reshape(2, count_rows, H * HD))

def attend(query_rows, grad_rows, key_rows, value_rows, key_live):
    score_scale = 1.0 / math.sqrt(HD)
    qpart = query_rows.reshape(-1, H, HD)
    gpart = grad_rows.reshape(-1, H, HD)
    kpart = key_rows.reshape(-1, H, HD)
    vpart = value_rows.reshape(-1, H, HD)
    scores = jnp.einsum('qhd,khd->hqk', qpart, kpart, precision=HIGH) * score_scale
    scores = jnp.where(key_live[None, None, :], scores, NEG)
    largest = lax.optimization_barrier(jnp.max(scores, axis=-1, keepdims=True))
    unnormed = jnp.exp(scores - largest)
    attn_probs = unnormed / lax.optimization_barrier(jnp.sum(unnormed, axis=-1, keepdims=True))
    probs_low = lax.optimization_barrier(attn_probs.astype(jnp.bfloat16)).astype(jnp.float32)
    output = jnp.einsum('hqk,khd->qhd', probs_low, vpart, precision=HIGH)
    prob_grad = jnp.einsum('qhd,khd->hqk', gpart, vpart, precision=HIGH)
    row_delta = lax.optimization_barrier(jnp.sum(attn_probs * prob_grad, axis=-1, keepdims=True))
    score_grad = attn_probs * (prob_grad - row_delta) * score_scale
    score_grad = lax.optimization_barrier(score_grad.astype(jnp.bfloat16)).astype(jnp.float32)
    query_grad = jnp.einsum('hqk,khd->qhd', score_grad, kpart, precision=HIGH)
    key_grad = jnp.einsum('hqk,qhd->khd', score_grad, qpart, precision=HIGH)
    value_grad = jnp.einsum('hqk,qhd->khd', probs_low, gpart, precision=HIGH)
    return (output.reshape(-1, D), query_grad.reshape(-1, D), key_grad.reshape(-1, D), value_grad.reshape(-1, D))

def reference(queries, keys, values, out_grad):
    stacked_kv = jnp.stack([keys, values]).astype(jnp.float32)
    near_all, near_pull = jax.vjp(lambda t: summarize(t, P1), stacked_kv)
    group_all, group_pull = jax.vjp(lambda t: summarize(t, P2), stacked_kv)
    top_all, top_pull = jax.vjp(lambda t: summarize(t, RATIO), group_all)
    blocks = FRAMES // BLOCK
    group_blocks = FR_DEV * N_SEQ // BLOCK
    near_ext = jnp.pad(near_all, ((0, 0), (NEAR, NEAR), (0, 0)))
    query_full = queries.astype(jnp.float32)
    grad_full = out_grad.astype(jnp.float32)
    position = jnp.arange(KEYS, dtype=jnp.int32)
    in_before = jnp.logical_and(position >= BLOCK, position < BLOCK + NEAR)
    in_after = jnp.logical_and(position >= BLOCK + NEAR, position < BLOCK + 2 * NEAR)

    def step(totals, block_index):
        group_grad, top_grad = totals
        offset = block_index * BLOCK
        query_rows = lax.dynamic_slice_in_dim(query_full, offset, BLOCK, 0)
        grad_rows = lax.dynamic_slice_in_dim(grad_full, offset, BLOCK, 0)
        diagonal = lax.dynamic_slice_in_dim(stacked_kv, offset, BLOCK, 1)
        before_rows = lax.dynamic_slice_in_dim(near_ext, block_index * NEAR, NEAR, 1)
        after_rows = lax.dynamic_slice_in_dim(near_ext, (block_index + 2) * NEAR, NEAR, 1)
        member = block_index // group_blocks
        group_rows = lax.dynamic_slice_in_dim(group_all, member * GROUP_ROWS, GROUP_ROWS, 1)
        key_sets = jnp.concatenate([diagonal, before_rows, after_rows, group_rows, top_all], axis=1)
        key_live = jnp.logical_not(jnp.logical_or(jnp.logical_and(in_before, block_index == 0), jnp.logical_and(in_after, block_index == blocks - 1)))
        output, query_grad, key_grad, value_grad = attend(query_rows, grad_rows, key_sets[0], key_sets[1], key_live)
        pair_grad = jnp.stack([key_grad, value_grad])
        lower = BLOCK + 2 * NEAR
        old_group = lax.dynamic_slice_in_dim(group_grad, member * GROUP_ROWS, GROUP_ROWS, 1)
        group_grad = lax.dynamic_update_slice_in_dim(group_grad, old_group + pair_grad[:, lower:lower + GROUP_ROWS], member * GROUP_ROWS, 1)
        top_grad = top_grad + pair_grad[:, lower + GROUP_ROWS:]
        outs = (output.astype(jnp.bfloat16), query_grad.astype(jnp.bfloat16), pair_grad[:, :BLOCK], pair_grad[:, BLOCK:BLOCK + NEAR], pair_grad[:, BLOCK + NEAR:BLOCK + 2 * NEAR])
        return ((group_grad, top_grad), outs)
    start_totals = (jnp.zeros((2, FRAMES // P2, D), jnp.float32), jnp.zeros((2, TOP_ROWS, D), jnp.float32))
    (group_grad, top_grad), stacked_outs = lax.scan(step, start_totals, jnp.arange(blocks, dtype=jnp.int32))
    attended_blocks, query_blocks, diag_grads, before_grads, after_grads = stacked_outs
    zero_pad = jnp.zeros((2, 2, NEAR, D), jnp.float32)
    ext_grads = jnp.concatenate([before_grads, zero_pad]) + jnp.concatenate([zero_pad, after_grads])
    near_grad = jnp.moveaxis(ext_grads[1:blocks + 1], 1, 0).reshape(2, FRAMES // P1, D)
    group_total = group_grad + top_pull(top_grad)[0]
    diag_total = jnp.moveaxis(diag_grads, 1, 0).reshape(2, FRAMES, D)
    kv_grad = diag_total + near_pull(near_grad)[0] + group_pull(group_total)[0]
    return (attended_blocks.reshape(FRAMES, D), query_blocks.reshape(FRAMES, D), kv_grad[0].astype(jnp.bfloat16), kv_grad[1].astype(jnp.bfloat16))
```

```python
import math

import jax
import jax.numpy as jnp
from jax import lax
from jax.experimental import pallas as pl
from jax.experimental.pallas import tpu as pltpu
from jax.sharding import PartitionSpec as P

H = 16
HD = 64
BLOCK = 512
P1 = 4
P2 = 32
RATIO = 8


EPS = 1e-06
NEG = -1e30


def extended(cells, sides, width):
    for axis, dim in sides:
        count = lax.axis_size(axis)
        ends = count - 1
        head = lax.slice_in_dim(cells, 0, width, axis=dim)
        tail = lax.slice_in_dim(cells, cells.shape[dim] - width, cells.shape[dim], axis=dim)
        cells = jnp.concatenate(
            [
                lax.ppermute(tail, axis, [(i, (i + 1) % count) for i in range(ends)]),
                cells,
                lax.ppermute(head, axis, [((i + 1) % count, i) for i in range(ends)]),
            ],
            axis=dim,
        )
    return cells


def shifted(block, axis, distance):
    devices = range(lax.axis_size(axis))
    route = [(i - distance, i) for i in devices if i - distance in devices]
    return lax.ppermute(block, axis, route)


def keep_bf16(value):
    rounded = lax.optimization_barrier(value.astype(jnp.bfloat16)).astype(jnp.float32)
    return value + lax.stop_gradient(rounded - value)


def pool_rows(stacked, factor):
    count_rows = stacked.shape[1] // factor
    return jnp.mean(
        stacked.reshape(2, count_rows, factor, stacked.shape[2]), axis=2, dtype=jnp.float32
    )


def normalize(pooled):
    shaped = pooled.reshape(pooled.shape[:-1] + (H, HD))
    scaled = shaped * lax.rsqrt(jnp.mean(shaped * shaped, axis=-1, keepdims=True) + EPS)
    return keep_bf16(scaled.reshape(pooled.shape))


def summary_back(pooled, upstream, factor):
    unused, pullback = jax.vjp(normalize, pooled)
    return jnp.repeat(pullback(upstream)[0] / factor, factor, axis=1)


PAIR = 2 * HD
CHUNK = 256


def dot(left, right):
    return jnp.dot(left, right, preferred_element_type=jnp.float32)


def attend_pair(lanes, live, query_ref, grad_ref, set_ref, score_ref, prob_ref, sgrad_ref):
    rows = query_ref.shape[0]
    count = set_ref.shape[1]
    spans = [(start, min(start + CHUNK, count)) for start in range(0, count, CHUNK)]
    query = query_ref[:, lanes].astype(jnp.float32) * (1.0 / math.sqrt(HD))
    query_t = query.T.astype(jnp.bfloat16)
    grad_t = grad_ref[:, lanes].astype(jnp.float32).T
    key_t = set_ref[0, :, lanes].T
    value_t = set_ref[1, :, lanes].T
    ones = jnp.ones((16, count), jnp.bfloat16)
    blank = jnp.zeros((HD, rows), jnp.bfloat16)
    outs, query_grads, scaled = [], [], []
    for head in range(2):
        part = slice(head * HD, (head + 1) * HD)

        def pad(half):
            return jnp.concatenate([half, blank] if head == 0 else [blank, half], axis=0)

        query_pad = pad(query_t[part])
        largest = None
        for start, stop in spans:
            scores = dot(set_ref[0, start:stop, lanes], query_pad)
            if start == BLOCK:
                scores = jnp.where(live, scores, NEG)
            score_ref[start:stop] = scores
            top = jnp.max(scores, axis=0, keepdims=True)
            largest = top if largest is None else jnp.maximum(largest, top)
        for start, stop in spans:
            prob_ref[head, start:stop] = jnp.exp(score_ref[start:stop] - largest).astype(
                jnp.bfloat16
            )
        mixed = dot(jnp.concatenate([value_t[part], ones], axis=0), prob_ref[head])
        inverse = 1.0 / mixed[HD : HD + 1]
        out = mixed[:HD] * inverse
        grad_scaled = (grad_t[part] * inverse).astype(jnp.bfloat16)
        delta = jnp.sum(grad_scaled.astype(jnp.float32) * out, axis=0, keepdims=True)
        grad_pad = pad(grad_scaled)
        for start, stop in spans:
            prob_grad = dot(set_ref[1, start:stop, lanes], grad_pad)
            sgrad_ref[head, start:stop] = prob_ref[head, start:stop] * (
                prob_grad - delta
            ).astype(jnp.bfloat16)
        outs.append(out)
        scaled.append(grad_scaled)
        query_grads.append(dot(key_t[part], sgrad_ref[head]) * (1.0 / math.sqrt(HD)))
    output = jnp.concatenate(outs, axis=0).T.astype(jnp.bfloat16)
    query_grad = jnp.concatenate(query_grads, axis=0).T.astype(jnp.bfloat16)
    grad_rows = jnp.concatenate(scaled, axis=0).astype(jnp.float32).T
    lower = lax.broadcasted_iota(jnp.int32, (rows, PAIR), 1) < HD

    def split(matrix):
        return (
            jnp.where(lower, matrix, 0.0).astype(jnp.bfloat16),
            jnp.where(lower, 0.0, matrix).astype(jnp.bfloat16),
        )

    grad_halves = split(grad_rows)
    query_halves = split(query)

    def row_grads(start, stop):
        key_grad = dot(sgrad_ref[0, start:stop], query_halves[0]) + dot(
            sgrad_ref[1, start:stop], query_halves[1]
        )
        value_grad = dot(prob_ref[0, start:stop], grad_halves[0]) + dot(
            prob_ref[1, start:stop], grad_halves[1]
        )
        return key_grad, value_grad

    return output, query_grad, row_grads, spans


def live_rows(number, total):
    row = lax.broadcasted_iota(jnp.int32, (CHUNK, 1), 0)
    before = row < CHUNK // 2
    dead = jnp.logical_or(
        jnp.logical_and(before, number == 0),
        jnp.logical_and(jnp.logical_not(before), number == total - 1),
    )
    return jnp.logical_not(dead)


def attend_kernel(
    query_ref, grad_ref, set_ref, out_ref, query_grad_ref, set_grad_ref,
    score_ref, prob_ref, sgrad_ref,
):
    seq_count = lax.axis_size("seq")
    number = lax.axis_index("grp") * seq_count + lax.axis_index("seq")
    live = live_rows(number, seq_count * lax.axis_size("grp"))

    def one_pair(pair, carry):
        lanes = pl.ds(pl.multiple_of(pair * PAIR, PAIR), PAIR)
        output, query_grad, row_grads, spans = attend_pair(
            lanes, live, query_ref, grad_ref, set_ref, score_ref, prob_ref, sgrad_ref
        )
        out_ref[:, lanes] = output
        query_grad_ref[:, lanes] = query_grad
        for start, stop in spans:
            key_grad, value_grad = row_grads(start, stop)
            set_grad_ref[0, start:stop, lanes] = key_grad
            set_grad_ref[1, start:stop, lanes] = value_grad
        return carry

    lax.fori_loop(0, query_ref.shape[1] // PAIR, one_pair, 0)


def attend_block(queries, out_grad, key_sets):
    rows, width = queries.shape
    count = key_sets.shape[1]
    whole = pl.BlockSpec(memory_space=pltpu.VMEM)
    return pl.pallas_call(
        attend_kernel,
        out_shape=(
            jax.ShapeDtypeStruct((rows, width), jnp.bfloat16),
            jax.ShapeDtypeStruct((rows, width), jnp.bfloat16),
            jax.ShapeDtypeStruct((2, count, width), jnp.float32),
        ),
        in_specs=[whole] * 3,
        out_specs=(whole,) * 3,
        scratch_shapes=[
            pltpu.VMEM((count, rows), jnp.float32),
            pltpu.VMEM((2, count, rows), jnp.bfloat16),
            pltpu.VMEM((2, count, rows), jnp.bfloat16),
        ],
        compiler_params=pltpu.CompilerParams(vmem_limit_bytes=56 * 2**20),
    )(queries, out_grad, key_sets)


def per_device(queries, keys, values, out_grad):
    frames = queries.shape[0]
    width_all = queries.shape[1]
    blocks = frames // BLOCK
    near_len = BLOCK // P1
    seq_count = lax.axis_size("seq")
    grp_count = lax.axis_size("grp")
    device = lax.axis_index("grp") * seq_count + lax.axis_index("seq")
    total_blocks = blocks * seq_count * grp_count
    stacked_kv = jnp.stack([keys, values])
    near_pooled = pool_rows(stacked_kv, P1)
    near_local = normalize(near_pooled).astype(jnp.bfloat16)
    near_ext = extended(near_local, ((("grp", "seq"), 1),), near_len)
    group_pooled = pool_rows(stacked_kv, P2)
    group_local = normalize(group_pooled).astype(jnp.bfloat16)
    group_all = lax.all_gather(group_local, "seq", axis=1, tiled=True)
    top_pooled = pool_rows(group_local, RATIO)
    top_local = normalize(top_pooled).astype(jnp.bfloat16)
    top_all = lax.all_gather(top_local, ("grp", "seq"), axis=1, tiled=True)
    group_len = group_all.shape[1]
    top_len = top_all.shape[1]
    key_count = BLOCK + 2 * near_len + group_len + top_len
    lower = BLOCK + 2 * near_len
    key_sets = jnp.concatenate(
        [stacked_kv, near_ext[:, :near_len], near_ext[:, 2 * near_len :], group_all, top_all],
        axis=1,
    )
    attended, query_grad, pair_grad = attend_block(queries, out_grad, key_sets)
    group_grad = pair_grad[:, lower : lower + group_len]
    top_grad = pair_grad[:, lower + group_len :]
    diag_total = pair_grad[:, :BLOCK]
    lower_rim = pair_grad[:, BLOCK : BLOCK + near_len]
    upper_rim = pair_grad[:, BLOCK + near_len : lower]
    from_next = shifted(lower_rim.astype(jnp.bfloat16), ("grp", "seq"), -1).astype(jnp.float32)
    from_prev = shifted(upper_rim.astype(jnp.bfloat16), ("grp", "seq"), 1).astype(jnp.float32)
    near_grad = from_next + from_prev
    top_own = lax.psum_scatter(top_grad, ("grp", "seq"), scatter_dimension=1, tiled=True)
    extra = summary_back(top_pooled, top_own, RATIO)
    group_own = (
        lax.psum_scatter(
            group_grad.astype(jnp.bfloat16), "seq", scatter_dimension=1, tiled=True
        ).astype(jnp.float32)
        + extra
    )
    kv_grad = (
        diag_total
        + summary_back(near_pooled, near_grad, P1)
        + summary_back(group_pooled, group_own, P2)
    )
    return (
        attended,
        query_grad,
        kv_grad[0].astype(jnp.bfloat16),
        kv_grad[1].astype(jnp.bfloat16),
    )


def solution(mesh):
    in_specs = (
        P(("grp", "seq"), None),
        P(("grp", "seq"), None),
        P(("grp", "seq"), None),
        P(("grp", "seq"), None),
    )
    out_specs = (
        P(("grp", "seq"), None),
        P(("grp", "seq"), None),
        P(("grp", "seq"), None),
        P(("grp", "seq"), None),
    )
    return jax.shard_map(
        per_device, mesh=mesh, in_specs=in_specs, out_specs=out_specs, check_vma=False
    )
```

```python
import functools
import math

import jax
import jax.numpy as jnp
from jax import lax
from jax.experimental import pallas as pl
from jax.experimental.pallas import tpu as pltpu
from jax.sharding import PartitionSpec as P

HD = 64
BLOCK = 512
P1 = 4
P2 = 32
RATIO = 8
NEAR = BLOCK // P1
OWN = BLOCK // P2
SUMS = NEAR + OWN
GROUP_BASE = BLOCK + 2 * NEAR

EPS = 1e-06
NEG = -1e30
WIDTH = 256
MESH = pl.DeviceIdType.MESH
NEAR_F, GROUP_F, TOP_F, NEAR_B, GROUP_B, TOP_B = range(6)


PAIR = 2 * HD
CHUNK = 256


def dot(left, right):
    return jnp.dot(left, right, preferred_element_type=jnp.float32)


def attend_pair(lanes, live, query_ref, grad_ref, set_ref, score_ref, prob_ref, sgrad_ref):
    rows = query_ref.shape[0]
    count = set_ref.shape[1]
    spans = [(start, min(start + CHUNK, count)) for start in range(0, count, CHUNK)]
    query = query_ref[:, lanes].astype(jnp.float32) * (1.0 / math.sqrt(HD))
    query_t = query.T.astype(jnp.bfloat16)
    grad_t = grad_ref[:, lanes].astype(jnp.float32).T
    key_t = set_ref[0, :, lanes].T
    value_t = set_ref[1, :, lanes].T
    ones = jnp.ones((16, count), jnp.bfloat16)
    blank = jnp.zeros((HD, rows), jnp.bfloat16)
    outs, query_grads, scaled = [], [], []
    for head in range(2):
        part = slice(head * HD, (head + 1) * HD)

        def pad(half):
            return jnp.concatenate([half, blank] if head == 0 else [blank, half], axis=0)

        query_pad = pad(query_t[part])
        largest = None
        for start, stop in spans:
            scores = dot(set_ref[0, start:stop, lanes], query_pad)
            if start == BLOCK:
                scores = jnp.where(live, scores, NEG)
            score_ref[start:stop] = scores
            top = jnp.max(scores, axis=0, keepdims=True)
            largest = top if largest is None else jnp.maximum(largest, top)
        for start, stop in spans:
            prob_ref[head, start:stop] = jnp.exp(score_ref[start:stop] - largest).astype(
                jnp.bfloat16
            )
        mixed = dot(jnp.concatenate([value_t[part], ones], axis=0), prob_ref[head])
        inverse = 1.0 / mixed[HD : HD + 1]
        out = mixed[:HD] * inverse
        grad_scaled = (grad_t[part] * inverse).astype(jnp.bfloat16)
        delta = jnp.sum(grad_scaled.astype(jnp.float32) * out, axis=0, keepdims=True)
        grad_pad = pad(grad_scaled)
        for start, stop in spans:
            prob_grad = dot(set_ref[1, start:stop, lanes], grad_pad)
            sgrad_ref[head, start:stop] = prob_ref[head, start:stop] * (
                prob_grad - delta
            ).astype(jnp.bfloat16)
        outs.append(out)
        scaled.append(grad_scaled)
        query_grads.append(dot(key_t[part], sgrad_ref[head]) * (1.0 / math.sqrt(HD)))
    output = jnp.concatenate(outs, axis=0).T.astype(jnp.bfloat16)
    query_grad = jnp.concatenate(query_grads, axis=0).T.astype(jnp.bfloat16)
    grad_rows = jnp.concatenate(scaled, axis=0).astype(jnp.float32).T
    lower = lax.broadcasted_iota(jnp.int32, (rows, PAIR), 1) < HD

    def split(matrix):
        return (
            jnp.where(lower, matrix, 0.0).astype(jnp.bfloat16),
            jnp.where(lower, 0.0, matrix).astype(jnp.bfloat16),
        )

    grad_halves = split(grad_rows)
    query_halves = split(query)

    def row_grads(start, stop):
        key_grad = dot(sgrad_ref[0, start:stop], query_halves[0]) + dot(
            sgrad_ref[1, start:stop], query_halves[1]
        )
        value_grad = dot(prob_ref[0, start:stop], grad_halves[0]) + dot(
            prob_ref[1, start:stop], grad_halves[1]
        )
        return key_grad, value_grad

    return output, query_grad, row_grads, spans


def live_rows(number, total):
    row = lax.broadcasted_iota(jnp.int32, (CHUNK, 1), 0)
    before = row < CHUNK // 2
    dead = jnp.logical_or(
        jnp.logical_and(before, number == 0),
        jnp.logical_and(jnp.logical_not(before), number == total - 1),
    )
    return jnp.logical_not(dead)


def head_mean(matrix):
    width = matrix.shape[1]
    row = lax.broadcasted_iota(jnp.int32, (width, width), 0)
    column = lax.broadcasted_iota(jnp.int32, (width, width), 1)
    block = jnp.where((row >> 6) == (column >> 6), 1.0 / HD, 0.0).astype(jnp.float32)
    return jnp.dot(
        matrix, block, preferred_element_type=jnp.float32, precision=lax.Precision.HIGHEST
    )


def normalize(pooled):
    root = lax.rsqrt(head_mean(pooled * pooled) + EPS)
    return pooled * root, root


def pull_back(unit, root, upstream):
    return root * (upstream - unit * head_mean(unit * upstream))


def pool_matrix(transposed):
    shape = (BLOCK, SUMS) if transposed else (SUMS, BLOCK)
    summary = lax.broadcasted_iota(jnp.int32, shape, 1 if transposed else 0)
    frame = lax.broadcasted_iota(jnp.int32, shape, 0 if transposed else 1)
    near = jnp.where((frame >> 2) == summary, 1.0 / P1, 0.0)
    group = jnp.where((frame >> 5) == summary - NEAR, 1.0 / P2, 0.0)
    return jnp.where(summary < NEAR, near, group).astype(jnp.bfloat16)


def top_matrix(tops, transposed):
    shape = (tops * RATIO, tops) if transposed else (tops, tops * RATIO)
    summary = lax.broadcasted_iota(jnp.int32, shape, 1 if transposed else 0)
    member = lax.broadcasted_iota(jnp.int32, shape, 0 if transposed else 1)
    return jnp.where((member >> 3) == summary, 1.0 / RATIO, 0.0).astype(jnp.bfloat16)


def layer_kernel(
    grp_count, seq_count,
    query_ref, key_ref, value_ref, grad_ref,
    out_ref, query_grad_ref, key_grad_ref, value_grad_ref,
    set_ref, near_ref, unit_ref, root_ref, top_unit_ref, top_root_ref,
    score_ref, prob_ref, sgrad_ref, diag_ref, group_sum_ref,
    near_out, near_in, group_out, group_in, top_out, top_in,
    send_sem, recv_sem,
):
    grp, seq = lax.axis_index("grp"), lax.axis_index("seq")
    total = grp_count * seq_count
    number = grp * seq_count + seq
    after, before = lax.rem(number + 1, total), lax.rem(number + total - 1, total)
    after_id = (after // seq_count, lax.rem(after, seq_count))
    before_id = (before // seq_count, lax.rem(before, seq_count))
    seq_peers = [lax.rem(seq + step, seq_count) for step in range(1, seq_count)]
    grp_peers = [lax.rem(grp + step, grp_count) for step in range(1, grp_count)]
    tops = 2 * seq_count
    top_base = GROUP_BASE + OWN * seq_count
    parts = query_ref.shape[1] // WIDTH
    live = live_rows(number, total)
    sources = (key_ref, value_ref)

    everyone = [after_id, before_id]
    everyone += [(grp, peer) for peer in seq_peers] + [(peer, seq) for peer in grp_peers]
    barrier = pltpu.get_barrier_semaphore()
    for peer in everyone:
        pl.semaphore_signal(barrier, inc=1, device_id=peer, device_id_type=MESH)

    def cols_of(part):
        return pl.ds(pl.multiple_of(part * WIDTH, WIDTH), WIDTH)

    def rows_of(start, step, index):
        return pl.ds(pl.multiple_of(start + index * step, step), step)

    def send(kind, part, source, target, peer):
        pltpu.make_async_remote_copy(
            src_ref=source,
            dst_ref=target,
            send_sem=send_sem.at[kind, part],
            recv_sem=recv_sem.at[kind, part],
            device_id=peer,
            device_id_type=MESH,
        ).start()

    def wait(kind, part, sems):
        cols = cols_of(part)
        if kind == NEAR_F:
            view = set_ref.at[:, BLOCK:GROUP_BASE, cols]
        elif kind == GROUP_F:
            view = set_ref.at[:, GROUP_BASE : GROUP_BASE + OWN * (seq_count - 1), cols]
        elif kind == TOP_F:
            view = set_ref.at[:, top_base : top_base + tops * (grp_count - 1), cols]
        else:
            view = {NEAR_B: near_in, GROUP_B: group_in, TOP_B: top_in}[kind]
            view = view.at[:, :, :, cols]
        pltpu.make_async_copy(view, view, sems.at[kind, part]).wait()

    pool = pool_matrix(False)

    def summarize_part(part, carry):
        cols = cols_of(part)
        own = rows_of(GROUP_BASE, OWN, seq)
        for side in range(2):
            rows = sources[side][:, cols]
            set_ref[side, :BLOCK, cols] = rows
            unit, root = normalize(dot(pool, rows))
            unit_ref[side, :, cols] = unit
            root_ref[side, :, cols] = root
            near_ref[side, :, cols] = unit[:NEAR].astype(jnp.bfloat16)
            set_ref[side, own, cols] = unit[NEAR:].astype(jnp.bfloat16)

        @pl.when(part == 0)
        def _():
            pl.semaphore_wait(barrier, len(everyone))

        for peer in seq_peers:
            block = set_ref.at[:, own, cols]
            send(GROUP_F, part, block, block, (grp, peer))
        block = near_ref.at[:, :, cols]
        send(NEAR_F, part, block, set_ref.at[:, BLOCK : BLOCK + NEAR, cols], after_id)
        send(NEAR_F, part, block, set_ref.at[:, BLOCK + NEAR : GROUP_BASE, cols], before_id)
        return carry

    def top_part(part, carry):
        cols = cols_of(part)
        mine = rows_of(top_base, tops, grp)
        wait(GROUP_F, part, recv_sem)
        matrix = top_matrix(tops, False)
        for side in range(2):
            unit, root = normalize(dot(matrix, set_ref[side, GROUP_BASE:top_base, cols]))
            top_unit_ref[side, :, cols] = unit
            top_root_ref[side, :, cols] = root
            set_ref[side, mine, cols] = unit.astype(jnp.bfloat16)
        for peer in grp_peers:
            block = set_ref.at[:, mine, cols]
            send(TOP_F, part, block, block, (peer, seq))
        return carry

    def attend_part(part):
        cols = cols_of(part)
        wait(NEAR_F, part, recv_sem)
        wait(TOP_F, part, recv_sem)

        def one_pair(pair, carry):
            lanes = pl.ds(pl.multiple_of(part * WIDTH + pair * PAIR, PAIR), PAIR)
            output, query_grad, row_grads, spans = attend_pair(
                lanes, live, query_ref, grad_ref, set_ref, score_ref, prob_ref, sgrad_ref
            )
            out_ref[:, lanes] = output
            query_grad_ref[:, lanes] = query_grad
            for start, stop in spans:
                both = row_grads(start, stop)
                for side in range(2):
                    rows = both[side]
                    if stop <= BLOCK:
                        diag_ref[side, start:stop, lanes] = rows
                    elif stop <= GROUP_BASE:
                        near_out[0, side, :, lanes] = rows[:NEAR].astype(jnp.bfloat16)
                        near_out[1, side, :, lanes] = rows[NEAR:].astype(jnp.bfloat16)
                    else:
                        cut = max(0, min(stop, top_base) - start)
                        if cut:
                            low = start - GROUP_BASE
                            group_sum_ref[side, low : low + cut, lanes] = rows[:cut]
                        if start + cut < stop:
                            low, high = start + cut - top_base, stop - top_base
                            top_out[side, low:high, lanes] = rows[cut:].astype(jnp.bfloat16)
            return carry

        lax.fori_loop(0, WIDTH // PAIR, one_pair, 0)
        for slot, peer in enumerate(grp_peers):
            block = top_out.at[:, rows_of(0, tops, peer), cols]
            send(TOP_B, part, block, top_in.at[slot, :, :, cols], (peer, seq))
        send(NEAR_B, part, near_out.at[0, :, :, cols], near_in.at[0, :, :, cols], before_id)
        send(NEAR_B, part, near_out.at[1, :, :, cols], near_in.at[1, :, :, cols], after_id)

    def group_part(part):
        cols = cols_of(part)
        wait(TOP_B, part, recv_sem)
        spread = top_matrix(tops, True)
        for side in range(2):
            upstream = top_out[side, rows_of(0, tops, grp), cols].astype(jnp.float32)
            for slot in range(grp_count - 1):
                upstream += top_in[slot, side, :, cols].astype(jnp.float32)
            back = pull_back(top_unit_ref[side, :, cols], top_root_ref[side, :, cols], upstream)
            group_out[side, :, cols] = (
                group_sum_ref[side, :, cols] + dot(spread, back.astype(jnp.bfloat16))
            ).astype(jnp.bfloat16)
        for slot, peer in enumerate(seq_peers):
            block = group_out.at[:, rows_of(0, OWN, peer), cols]
            send(GROUP_B, part, block, group_in.at[slot, :, :, cols], (grp, peer))

    def final_part(part):
        cols = cols_of(part)
        wait(NEAR_B, part, recv_sem)
        wait(GROUP_B, part, recv_sem)
        spread = pool_matrix(True)
        for side, result in enumerate((key_grad_ref, value_grad_ref)):
            near = near_in[0, side, :, cols].astype(jnp.float32)
            near += near_in[1, side, :, cols].astype(jnp.float32)
            group = group_out[side, rows_of(0, OWN, seq), cols].astype(jnp.float32)
            for slot in range(seq_count - 1):
                group += group_in[slot, side, :, cols].astype(jnp.float32)
            upstream = jnp.concatenate([near, group], axis=0)
            back = pull_back(unit_ref[side, :, cols], root_ref[side, :, cols], upstream)
            result[:, cols] = (
                diag_ref[side, :, cols] + dot(spread, back.astype(jnp.bfloat16))
            ).astype(jnp.bfloat16)

    lax.fori_loop(0, parts, summarize_part, 0)
    lax.fori_loop(0, parts, top_part, 0)

    def stage(index, carry):
        @pl.when(index < parts)
        def _():
            attend_part(index)

        @pl.when(jnp.logical_and(index >= 1, index <= parts))
        def _():
            group_part(index - 1)

        @pl.when(index >= 2)
        def _():
            final_part(index - 2)

        return carry

    lax.fori_loop(0, parts + 2, stage, 0)
    for part in range(parts):
        for kind in range(6):
            wait(kind, part, send_sem)


def per_device(grp_count, seq_count, queries, keys, values, out_grad):
    rows, width = queries.shape
    group_rows = OWN * seq_count
    tops = 2 * seq_count
    count = GROUP_BASE + group_rows + tops * grp_count
    parts = width // WIDTH
    whole = pl.BlockSpec(memory_space=pltpu.VMEM)
    shape = jax.ShapeDtypeStruct((rows, width), jnp.bfloat16)
    low, high = jnp.bfloat16, jnp.float32
    return pl.pallas_call(
        functools.partial(layer_kernel, grp_count, seq_count),
        out_shape=(shape,) * 4,
        in_specs=[whole] * 4,
        out_specs=(whole,) * 4,
        scratch_shapes=[
            pltpu.VMEM((2, count, width), low),
            pltpu.VMEM((2, NEAR, width), low),
            pltpu.VMEM((2, SUMS, width), high),
            pltpu.VMEM((2, SUMS, width), high),
            pltpu.VMEM((2, tops, width), high),
            pltpu.VMEM((2, tops, width), high),
            pltpu.VMEM((count, rows), high),
            pltpu.VMEM((2, count, rows), low),
            pltpu.VMEM((2, count, rows), low),
            pltpu.VMEM((2, rows, width), high),
            pltpu.VMEM((2, group_rows, width), high),
            pltpu.VMEM((2, 2, NEAR, width), low),
            pltpu.VMEM((2, 2, NEAR, width), low),
            pltpu.VMEM((2, group_rows, width), low),
            pltpu.VMEM((seq_count - 1, 2, OWN, width), low),
            pltpu.VMEM((2, tops * grp_count, width), low),
            pltpu.VMEM((grp_count - 1, 2, tops, width), low),
            pltpu.SemaphoreType.DMA((6, parts)),
            pltpu.SemaphoreType.DMA((6, parts)),
        ],
        compiler_params=pltpu.CompilerParams(
            vmem_limit_bytes=60 * 2**20, collective_id=0, has_side_effects=True
        ),
    )(queries, keys, values, out_grad)


def solution(mesh):
    spec = P(("grp", "seq"), None)
    return jax.shard_map(
        functools.partial(per_device, mesh.shape["grp"], mesh.shape["seq"]),
        mesh=mesh,
        in_specs=(spec,) * 4,
        out_specs=(spec,) * 4,
        check_vma=False,
    )
```

```python
import functools
import math

import jax
import jax.numpy as jnp
from jax import lax
from jax.experimental import pallas as pl
from jax.experimental.pallas import tpu as pltpu
from jax.sharding import PartitionSpec as P

HD = 64
BLOCK = 512
P1 = 4
P2 = 32
RATIO = 8
NEAR = BLOCK // P1
OWN = BLOCK // P2
SUMS = NEAR + OWN
GROUP_BASE = BLOCK + 2 * NEAR

EPS = 1e-06
NEG = -1e30
WIDTH = 256
MESH = pl.DeviceIdType.MESH
NEAR_F, GROUP_F, TOP_F, NEAR_B, GROUP_B, TOP_B = range(6)


PAIR = 2 * HD
CHUNK = 256


def dot(left, right):
    return jnp.dot(left, right, preferred_element_type=jnp.float32)


def attend_pair(lanes, live, query_ref, grad_ref, set_ref, score_ref, prob_ref, sgrad_ref):
    rows = query_ref.shape[0]
    count = set_ref.shape[1]
    spans = [(start, min(start + CHUNK, count)) for start in range(0, count, CHUNK)]
    query = query_ref[:, lanes].astype(jnp.float32) * (1.0 / math.sqrt(HD))
    query_t = query.T.astype(jnp.bfloat16)
    grad_t = grad_ref[:, lanes].astype(jnp.float32).T
    key_t = set_ref[0, :, lanes].T
    value_t = set_ref[1, :, lanes].T
    ones = jnp.ones((16, count), jnp.bfloat16)
    blank = jnp.zeros((HD, rows), jnp.bfloat16)
    outs, query_grads, scaled = [], [], []
    for head in range(2):
        part = slice(head * HD, (head + 1) * HD)

        def pad(half):
            return jnp.concatenate([half, blank] if head == 0 else [blank, half], axis=0)

        query_pad = pad(query_t[part])
        largest = None
        for start, stop in spans:
            scores = dot(set_ref[0, start:stop, lanes], query_pad)
            if start == BLOCK:
                scores = jnp.where(live, scores, NEG)
            score_ref[start:stop] = scores
            top = jnp.max(scores, axis=0, keepdims=True)
            largest = top if largest is None else jnp.maximum(largest, top)
        for start, stop in spans:
            prob_ref[head, start:stop] = jnp.exp(score_ref[start:stop] - largest).astype(
                jnp.bfloat16
            )
        mixed = dot(jnp.concatenate([value_t[part], ones], axis=0), prob_ref[head])
        inverse = 1.0 / mixed[HD : HD + 1]
        out = mixed[:HD] * inverse
        grad_scaled = (grad_t[part] * inverse).astype(jnp.bfloat16)
        delta = jnp.sum(grad_scaled.astype(jnp.float32) * out, axis=0, keepdims=True)
        grad_pad = pad(grad_scaled)
        for start, stop in spans:
            prob_grad = dot(set_ref[1, start:stop, lanes], grad_pad)
            sgrad_ref[head, start:stop] = prob_ref[head, start:stop] * (
                prob_grad - delta
            ).astype(jnp.bfloat16)
        outs.append(out)
        scaled.append(grad_scaled)
        query_grads.append(dot(key_t[part], sgrad_ref[head]) * (1.0 / math.sqrt(HD)))
    output = jnp.concatenate(outs, axis=0).T.astype(jnp.bfloat16)
    query_grad = jnp.concatenate(query_grads, axis=0).T.astype(jnp.bfloat16)
    grad_rows = jnp.concatenate(scaled, axis=0).astype(jnp.float32).T
    lower = lax.broadcasted_iota(jnp.int32, (rows, PAIR), 1) < HD

    def split(matrix):
        return (
            jnp.where(lower, matrix, 0.0).astype(jnp.bfloat16),
            jnp.where(lower, 0.0, matrix).astype(jnp.bfloat16),
        )

    grad_halves = split(grad_rows)
    query_halves = split(query)

    def row_grads(start, stop):
        key_grad = dot(sgrad_ref[0, start:stop], query_halves[0]) + dot(
            sgrad_ref[1, start:stop], query_halves[1]
        )
        value_grad = dot(prob_ref[0, start:stop], grad_halves[0]) + dot(
            prob_ref[1, start:stop], grad_halves[1]
        )
        return key_grad, value_grad

    return output, query_grad, row_grads, spans


def live_rows(number, total):
    row = lax.broadcasted_iota(jnp.int32, (CHUNK, 1), 0)
    before = row < CHUNK // 2
    dead = jnp.logical_or(
        jnp.logical_and(before, number == 0),
        jnp.logical_and(jnp.logical_not(before), number == total - 1),
    )
    return jnp.logical_not(dead)


def head_mean(matrix):
    width = matrix.shape[1]
    row = lax.broadcasted_iota(jnp.int32, (width, width), 0)
    column = lax.broadcasted_iota(jnp.int32, (width, width), 1)
    block = jnp.where((row >> 6) == (column >> 6), 1.0 / HD, 0.0).astype(jnp.bfloat16)
    high = matrix.astype(jnp.bfloat16)
    low = (matrix - high.astype(jnp.float32)).astype(jnp.bfloat16)
    return dot(high, block) + dot(low, block)


def normalize(pooled):
    root = lax.rsqrt(head_mean(pooled * pooled) + EPS)
    return pooled * root, root


def pull_back(unit, root, upstream):
    return root * (upstream - unit * head_mean(unit * upstream))


def pool_matrix(transposed):
    shape = (BLOCK, SUMS) if transposed else (SUMS, BLOCK)
    summary = lax.broadcasted_iota(jnp.int32, shape, 1 if transposed else 0)
    frame = lax.broadcasted_iota(jnp.int32, shape, 0 if transposed else 1)
    near = jnp.where((frame >> 2) == summary, 1.0 / P1, 0.0)
    group = jnp.where((frame >> 5) == summary - NEAR, 1.0 / P2, 0.0)
    return jnp.where(summary < NEAR, near, group).astype(jnp.bfloat16)


def top_matrix(tops, transposed):
    shape = (tops * RATIO, tops) if transposed else (tops, tops * RATIO)
    summary = lax.broadcasted_iota(jnp.int32, shape, 1 if transposed else 0)
    member = lax.broadcasted_iota(jnp.int32, shape, 0 if transposed else 1)
    return jnp.where((member >> 3) == summary, 1.0 / RATIO, 0.0).astype(jnp.bfloat16)


def layer_kernel(
    grp_count, seq_count,
    query_ref, key_ref, value_ref, grad_ref,
    out_ref, query_grad_ref, key_grad_ref, value_grad_ref,
    set_ref, near_ref, unit_ref, root_ref, top_unit_ref, top_root_ref,
    score_ref, prob_ref, sgrad_ref, diag_ref, group_sum_ref,
    near_out, near_in, group_out, group_in, top_out, top_in,
    send_sem, recv_sem,
):
    grp, seq = lax.axis_index("grp"), lax.axis_index("seq")
    total = grp_count * seq_count
    number = grp * seq_count + seq
    after, before = lax.rem(number + 1, total), lax.rem(number + total - 1, total)
    after_id = (after // seq_count, lax.rem(after, seq_count))
    before_id = (before // seq_count, lax.rem(before, seq_count))
    seq_peers = [lax.rem(seq + step, seq_count) for step in range(1, seq_count)]
    grp_peers = [lax.rem(grp + step, grp_count) for step in range(1, grp_count)]
    tops = 2 * seq_count
    top_base = GROUP_BASE + OWN * seq_count
    parts = query_ref.shape[1] // WIDTH
    live = live_rows(number, total)
    sources = (key_ref, value_ref)

    everyone = [after_id, before_id]
    everyone += [(grp, peer) for peer in seq_peers] + [(peer, seq) for peer in grp_peers]
    barrier = pltpu.get_barrier_semaphore()
    for peer in everyone:
        pl.semaphore_signal(barrier, inc=1, device_id=peer, device_id_type=MESH)

    def cols_of(part):
        return pl.ds(pl.multiple_of(part * WIDTH, WIDTH), WIDTH)

    def rows_of(start, step, index):
        return pl.ds(pl.multiple_of(start + index * step, step), step)

    def send(kind, part, source, target, peer):
        pltpu.make_async_remote_copy(
            src_ref=source,
            dst_ref=target,
            send_sem=send_sem.at[kind, part],
            recv_sem=recv_sem.at[kind, part],
            device_id=peer,
            device_id_type=MESH,
        ).start()

    def wait(kind, part, sems):
        cols = cols_of(part)
        if kind == NEAR_F:
            view = set_ref.at[:, BLOCK:GROUP_BASE, cols]
        elif kind == GROUP_F:
            view = set_ref.at[:, GROUP_BASE : GROUP_BASE + OWN * (seq_count - 1), cols]
        elif kind == TOP_F:
            view = set_ref.at[:, top_base : top_base + tops * (grp_count - 1), cols]
        else:
            view = {NEAR_B: near_in, GROUP_B: group_in, TOP_B: top_in}[kind]
            view = view.at[:, :, :, cols]
        pltpu.make_async_copy(view, view, sems.at[kind, part]).wait()

    pool = pool_matrix(False)

    def summarize_part(part, carry):
        cols = cols_of(part)
        own = rows_of(GROUP_BASE, OWN, seq)
        for side in range(2):
            rows = sources[side][:, cols]
            set_ref[side, :BLOCK, cols] = rows
            unit, root = normalize(dot(pool, rows))
            unit_ref[side, :, cols] = unit
            root_ref[side, :, cols] = root
            near_ref[side, :, cols] = unit[:NEAR].astype(jnp.bfloat16)
            set_ref[side, own, cols] = unit[NEAR:].astype(jnp.bfloat16)

        @pl.when(part == 0)
        def _():
            pl.semaphore_wait(barrier, len(everyone))

        for peer in seq_peers:
            block = set_ref.at[:, own, cols]
            send(GROUP_F, part, block, block, (grp, peer))
        @pl.when(part > 0)
        def _():
            send_near(part - 1)

        return carry

    def send_near(part):
        cols = cols_of(part)
        block = near_ref.at[:, :, cols]
        send(NEAR_F, part, block, set_ref.at[:, BLOCK : BLOCK + NEAR, cols], after_id)
        send(NEAR_F, part, block, set_ref.at[:, BLOCK + NEAR : GROUP_BASE, cols], before_id)

    def top_part(part):
        cols = cols_of(part)
        mine = rows_of(top_base, tops, grp)
        wait(GROUP_F, part, recv_sem)
        matrix = top_matrix(tops, False)
        for side in range(2):
            unit, root = normalize(dot(matrix, set_ref[side, GROUP_BASE:top_base, cols]))
            top_unit_ref[side, :, cols] = unit
            top_root_ref[side, :, cols] = root
            set_ref[side, mine, cols] = unit.astype(jnp.bfloat16)
        for peer in grp_peers:
            block = set_ref.at[:, mine, cols]
            send(TOP_F, part, block, block, (peer, seq))

    def attend_part(part):
        cols = cols_of(part)
        wait(NEAR_F, part, recv_sem)
        wait(TOP_F, part, recv_sem)

        def one_pair(pair, carry):
            @pl.when(jnp.logical_and(pair == 1, part >= 1))
            def _():
                group_part(part - 1)

            lanes = pl.ds(pl.multiple_of(part * WIDTH + pair * PAIR, PAIR), PAIR)
            output, query_grad, row_grads, spans = attend_pair(
                lanes, live, query_ref, grad_ref, set_ref, score_ref, prob_ref, sgrad_ref
            )
            out_ref[:, lanes] = output
            query_grad_ref[:, lanes] = query_grad
            for start, stop in spans:
                both = row_grads(start, stop)
                for side in range(2):
                    rows = both[side]
                    if stop <= BLOCK:
                        diag_ref[side, start:stop, lanes] = rows
                    elif stop <= GROUP_BASE:
                        near_out[0, side, :, lanes] = rows[:NEAR].astype(jnp.bfloat16)
                        near_out[1, side, :, lanes] = rows[NEAR:].astype(jnp.bfloat16)
                    else:
                        cut = max(0, min(stop, top_base) - start)
                        if cut:
                            low = start - GROUP_BASE
                            group_sum_ref[side, low : low + cut, lanes] = rows[:cut]
                        if start + cut < stop:
                            low, high = start + cut - top_base, stop - top_base
                            top_out[side, low:high, lanes] = rows[cut:].astype(jnp.bfloat16)
            for way, peer in enumerate((before_id, after_id)):
                source = near_out.at[way, :, :, lanes]
                send(NEAR_B, part, source, near_in.at[way, :, :, lanes], peer)
            return carry

        lax.fori_loop(0, WIDTH // PAIR, one_pair, 0)
        for slot, peer in enumerate(grp_peers):
            block = top_out.at[:, rows_of(0, tops, peer), cols]
            send(TOP_B, part, block, top_in.at[slot, :, :, cols], (peer, seq))

    def group_part(part):
        cols = cols_of(part)
        wait(TOP_B, part, recv_sem)
        spread = top_matrix(tops, True)
        for side in range(2):
            upstream = top_out[side, rows_of(0, tops, grp), cols].astype(jnp.float32)
            for slot in range(grp_count - 1):
                upstream += top_in[slot, side, :, cols].astype(jnp.float32)
            back = pull_back(top_unit_ref[side, :, cols], top_root_ref[side, :, cols], upstream)
            group_out[side, :, cols] = (
                group_sum_ref[side, :, cols] + dot(spread, back.astype(jnp.bfloat16))
            ).astype(jnp.bfloat16)
        for slot, peer in enumerate(seq_peers):
            block = group_out.at[:, rows_of(0, OWN, peer), cols]
            send(GROUP_B, part, block, group_in.at[slot, :, :, cols], (grp, peer))

    def final_part(part):
        cols = cols_of(part)
        wait(NEAR_B, part, recv_sem)
        wait(GROUP_B, part, recv_sem)
        spread = pool_matrix(True)
        for side, result in enumerate((key_grad_ref, value_grad_ref)):
            near = near_in[0, side, :, cols].astype(jnp.float32)
            near += near_in[1, side, :, cols].astype(jnp.float32)
            group = group_out[side, rows_of(0, OWN, seq), cols].astype(jnp.float32)
            for slot in range(seq_count - 1):
                group += group_in[slot, side, :, cols].astype(jnp.float32)
            upstream = jnp.concatenate([near, group], axis=0)
            back = pull_back(unit_ref[side, :, cols], root_ref[side, :, cols], upstream)
            result[:, cols] = (
                diag_ref[side, :, cols] + dot(spread, back.astype(jnp.bfloat16))
            ).astype(jnp.bfloat16)

    lax.fori_loop(0, parts, summarize_part, 0)
    send_near(parts - 1)
    top_part(0)

    def stage(index, carry):
        @pl.when(index + 1 < parts)
        def _():
            top_part(index + 1)

        @pl.when(index < parts)
        def _():
            attend_part(index)

        @pl.when(index == parts)
        def _():
            group_part(index - 1)

        @pl.when(index >= 2)
        def _():
            final_part(index - 2)

        return carry

    lax.fori_loop(0, parts + 2, stage, 0)
    for part in range(parts):
        for kind in range(6):
            wait(kind, part, send_sem)


def store_kernel(*refs):
    sems = refs[8]
    copies = [pltpu.make_async_copy(refs[i], refs[i + 4], sems.at[i]) for i in range(4)]
    for copy in copies:
        copy.start()
    for copy in copies:
        copy.wait()


def per_device(grp_count, seq_count, queries, keys, values, out_grad):
    rows, width = queries.shape
    group_rows = OWN * seq_count
    tops = 2 * seq_count
    count = GROUP_BASE + group_rows + tops * grp_count
    parts = width // WIDTH
    whole = pl.BlockSpec(memory_space=pltpu.VMEM)
    shape = jax.ShapeDtypeStruct((rows, width), jnp.bfloat16)
    low, high = jnp.bfloat16, jnp.float32
    results = pl.pallas_call(
        functools.partial(layer_kernel, grp_count, seq_count),
        out_shape=(shape,) * 4,
        in_specs=[whole] * 4,
        out_specs=(whole,) * 4,
        scratch_shapes=[
            pltpu.VMEM((2, count, width), low),
            pltpu.VMEM((2, NEAR, width), low),
            pltpu.VMEM((2, SUMS, width), high),
            pltpu.VMEM((2, SUMS, width), high),
            pltpu.VMEM((2, tops, width), high),
            pltpu.VMEM((2, tops, width), high),
            pltpu.VMEM((count, rows), high),
            pltpu.VMEM((2, count, rows), low),
            pltpu.VMEM((2, count, rows), low),
            pltpu.VMEM((2, rows, width), high),
            pltpu.VMEM((2, group_rows, width), high),
            pltpu.VMEM((2, 2, NEAR, width), low),
            pltpu.VMEM((2, 2, NEAR, width), low),
            pltpu.VMEM((2, group_rows, width), low),
            pltpu.VMEM((seq_count - 1, 2, OWN, width), low),
            pltpu.VMEM((2, tops * grp_count, width), low),
            pltpu.VMEM((grp_count - 1, 2, tops, width), low),
            pltpu.SemaphoreType.DMA((6, parts)),
            pltpu.SemaphoreType.DMA((6, parts)),
        ],
        compiler_params=pltpu.CompilerParams(
            vmem_limit_bytes=60 * 2**20, collective_id=0, has_side_effects=True
        ),
    )(queries, keys, values, out_grad)
    anywhere = pl.BlockSpec(memory_space=pltpu.HBM)
    return pl.pallas_call(
        store_kernel,
        out_shape=(shape,) * 4,
        in_specs=[anywhere] * 4,
        out_specs=(anywhere,) * 4,
        scratch_shapes=[pltpu.SemaphoreType.DMA((4,))],
    )(*results)


def solution(mesh):
    spec = P(("grp", "seq"), None)
    return jax.shard_map(
        functools.partial(per_device, mesh.shape["grp"], mesh.shape["seq"]),
        mesh=mesh,
        in_specs=(spec,) * 4,
        out_specs=(spec,) * 4,
        check_vma=False,
    )
```

```python
import functools
import math

import jax
import jax.numpy as jnp
from jax import lax
from jax.experimental import pallas as pl
from jax.experimental.pallas import tpu as pltpu
from jax.sharding import PartitionSpec as P

HD = 64
BLOCK = 512
P1 = 4
P2 = 32
RATIO = 8
NEAR = BLOCK // P1
OWN = BLOCK // P2
SUMS = NEAR + OWN
GROUP_BASE = BLOCK + 2 * NEAR

EPS = 1e-06
NEG = -1e30
WIDTH = 256
MESH = pl.DeviceIdType.MESH
NEAR_F, GROUP_F, TOP_F, NEAR_B, GROUP_B, TOP_B = range(6)


PAIR = 2 * HD
CHUNK = 256


def dot(left, right):
    return jnp.dot(left, right, preferred_element_type=jnp.float32)


def attend_pair(lanes, live, query_ref, grad_ref, set_ref, score_ref, prob_ref, sgrad_ref):
    rows = query_ref.shape[0]
    count = set_ref.shape[1]
    spans = [(start, min(start + CHUNK, count)) for start in range(0, count, CHUNK)]
    query = query_ref[:, lanes].astype(jnp.float32) * (1.0 / math.sqrt(HD))
    query_t = query.T.astype(jnp.bfloat16)
    grad_t = grad_ref[:, lanes].astype(jnp.float32).T
    key_t = set_ref[0, :, lanes].T
    value_t = set_ref[1, :, lanes].T
    ones = jnp.ones((16, count), jnp.bfloat16)
    blank = jnp.zeros((HD, rows), jnp.bfloat16)
    outs, query_grads, scaled = [], [], []
    for head in range(2):
        part = slice(head * HD, (head + 1) * HD)

        def pad(half):
            return jnp.concatenate([half, blank] if head == 0 else [blank, half], axis=0)

        query_pad = pad(query_t[part])
        largest = None
        for start, stop in spans:
            scores = dot(set_ref[0, start:stop, lanes], query_pad)
            if start == BLOCK:
                scores = jnp.where(live, scores, NEG)
            score_ref[start:stop] = scores
            top = jnp.max(scores, axis=0, keepdims=True)
            largest = top if largest is None else jnp.maximum(largest, top)
        for start, stop in spans:
            prob_ref[head, start:stop] = jnp.exp(score_ref[start:stop] - largest).astype(
                jnp.bfloat16
            )
        mixed = dot(jnp.concatenate([value_t[part], ones], axis=0), prob_ref[head])
        inverse = 1.0 / mixed[HD : HD + 1]
        out = mixed[:HD] * inverse
        grad_scaled = (grad_t[part] * inverse).astype(jnp.bfloat16)
        delta = jnp.sum(grad_scaled.astype(jnp.float32) * out, axis=0, keepdims=True)
        grad_pad = pad(grad_scaled)
        for start, stop in spans:
            prob_grad = dot(set_ref[1, start:stop, lanes], grad_pad)
            sgrad_ref[head, start:stop] = prob_ref[head, start:stop] * (
                prob_grad - delta
            ).astype(jnp.bfloat16)
        outs.append(out)
        scaled.append(grad_scaled)
        query_grads.append(dot(key_t[part], sgrad_ref[head]) * (1.0 / math.sqrt(HD)))
    output = jnp.concatenate(outs, axis=0).T.astype(jnp.bfloat16)
    query_grad = jnp.concatenate(query_grads, axis=0).T.astype(jnp.bfloat16)
    grad_rows = jnp.concatenate(scaled, axis=0).astype(jnp.float32).T
    lower = lax.broadcasted_iota(jnp.int32, (rows, PAIR), 1) < HD

    def split(matrix):
        return (
            jnp.where(lower, matrix, 0.0).astype(jnp.bfloat16),
            jnp.where(lower, 0.0, matrix).astype(jnp.bfloat16),
        )

    grad_halves = split(grad_rows)
    query_halves = split(query)

    def row_grads(start, stop):
        key_grad = dot(sgrad_ref[0, start:stop], query_halves[0]) + dot(
            sgrad_ref[1, start:stop], query_halves[1]
        )
        value_grad = dot(prob_ref[0, start:stop], grad_halves[0]) + dot(
            prob_ref[1, start:stop], grad_halves[1]
        )
        return key_grad, value_grad

    return output, query_grad, row_grads, spans


def live_rows(number, total):
    row = lax.broadcasted_iota(jnp.int32, (CHUNK, 1), 0)
    before = row < CHUNK // 2
    dead = jnp.logical_or(
        jnp.logical_and(before, number == 0),
        jnp.logical_and(jnp.logical_not(before), number == total - 1),
    )
    return jnp.logical_not(dead)


def head_mean(matrix):
    width = matrix.shape[1]
    row = lax.broadcasted_iota(jnp.int32, (width, width), 0)
    column = lax.broadcasted_iota(jnp.int32, (width, width), 1)
    block = jnp.where((row >> 6) == (column >> 6), 1.0 / HD, 0.0).astype(jnp.bfloat16)
    high = matrix.astype(jnp.bfloat16)
    low = (matrix - high.astype(jnp.float32)).astype(jnp.bfloat16)
    return dot(high, block) + dot(low, block)


def normalize(pooled):
    root = lax.rsqrt(head_mean(pooled * pooled) + EPS)
    return pooled * root, root


def pull_back(unit, root, upstream):
    return root * (upstream - unit * head_mean(unit * upstream))


def pool_matrix(transposed):
    shape = (BLOCK, SUMS) if transposed else (SUMS, BLOCK)
    summary = lax.broadcasted_iota(jnp.int32, shape, 1 if transposed else 0)
    frame = lax.broadcasted_iota(jnp.int32, shape, 0 if transposed else 1)
    near = jnp.where((frame >> 2) == summary, 1.0 / P1, 0.0)
    group = jnp.where((frame >> 5) == summary - NEAR, 1.0 / P2, 0.0)
    return jnp.where(summary < NEAR, near, group).astype(jnp.bfloat16)


def top_matrix(tops, transposed):
    shape = (tops * RATIO, tops) if transposed else (tops, tops * RATIO)
    summary = lax.broadcasted_iota(jnp.int32, shape, 1 if transposed else 0)
    member = lax.broadcasted_iota(jnp.int32, shape, 0 if transposed else 1)
    return jnp.where((member >> 3) == summary, 1.0 / RATIO, 0.0).astype(jnp.bfloat16)


def layer_kernel(
    grp_count, seq_count,
    query_ref, key_ref, value_ref, grad_ref,
    out_ref, query_grad_ref, key_grad_ref, value_grad_ref,
    set_ref, near_ref, unit_ref, root_ref, top_unit_ref, top_root_ref,
    score_ref, prob_ref, sgrad_ref, diag_ref, group_sum_ref,
    near_out, near_in, group_out, group_in, top_out, top_in,
    send_sem, recv_sem,
):
    grp, seq = lax.axis_index("grp"), lax.axis_index("seq")
    total = grp_count * seq_count
    number = grp * seq_count + seq
    after, before = lax.rem(number + 1, total), lax.rem(number + total - 1, total)
    after_id = (after // seq_count, lax.rem(after, seq_count))
    before_id = (before // seq_count, lax.rem(before, seq_count))
    seq_peers = [lax.rem(seq + step, seq_count) for step in range(1, seq_count)]
    grp_peers = [lax.rem(grp + step, grp_count) for step in range(1, grp_count)]
    tops = 2 * seq_count
    top_base = GROUP_BASE + OWN * seq_count
    parts = query_ref.shape[1] // WIDTH
    live = live_rows(number, total)
    sources = (key_ref, value_ref)

    everyone = [after_id, before_id]
    everyone += [(grp, peer) for peer in seq_peers] + [(peer, seq) for peer in grp_peers]
    barrier = pltpu.get_barrier_semaphore()
    for peer in everyone:
        pl.semaphore_signal(barrier, inc=1, device_id=peer, device_id_type=MESH)

    def cols_of(part):
        return pl.ds(pl.multiple_of(part * WIDTH, WIDTH), WIDTH)

    def rows_of(start, step, index):
        return pl.ds(pl.multiple_of(start + index * step, step), step)

    def send(kind, part, source, target, peer):
        pltpu.make_async_remote_copy(
            src_ref=source,
            dst_ref=target,
            send_sem=send_sem.at[kind, part],
            recv_sem=recv_sem.at[kind, part],
            device_id=peer,
            device_id_type=MESH,
        ).start()

    def wait(kind, part, sems):
        cols = cols_of(part)
        if kind == NEAR_F:
            view = set_ref.at[:, BLOCK:GROUP_BASE, cols]
        elif kind == GROUP_F:
            view = set_ref.at[:, GROUP_BASE : GROUP_BASE + OWN * (seq_count - 1), cols]
        elif kind == TOP_F:
            view = set_ref.at[:, top_base : top_base + tops * (grp_count - 1), cols]
        else:
            view = {NEAR_B: near_in, GROUP_B: group_in, TOP_B: top_in}[kind]
            view = view.at[:, :, :, cols]
        pltpu.make_async_copy(view, view, sems.at[kind, part]).wait()

    pool = pool_matrix(False)

    def summarize_part(part, carry):
        cols = cols_of(part)
        own = rows_of(GROUP_BASE, OWN, seq)
        for side in range(2):
            rows = sources[side][:, cols]
            set_ref[side, :BLOCK, cols] = rows
            unit, root = normalize(dot(pool, rows))
            unit_ref[side, :, cols] = unit
            root_ref[side, :, cols] = root
            near_ref[side, :, cols] = unit[:NEAR].astype(jnp.bfloat16)
            set_ref[side, own, cols] = unit[NEAR:].astype(jnp.bfloat16)

        @pl.when(part == 0)
        def _():
            pl.semaphore_wait(barrier, len(everyone))

        for peer in seq_peers:
            block = set_ref.at[:, own, cols]
            send(GROUP_F, part, block, block, (grp, peer))
        @pl.when(part > 0)
        def _():
            send_near(part - 1)

        return carry

    def send_near(part):
        cols = cols_of(part)
        block = near_ref.at[:, :, cols]
        send(NEAR_F, part, block, set_ref.at[:, BLOCK : BLOCK + NEAR, cols], after_id)
        send(NEAR_F, part, block, set_ref.at[:, BLOCK + NEAR : GROUP_BASE, cols], before_id)

    def top_part(part):
        cols = cols_of(part)
        mine = rows_of(top_base, tops, grp)
        wait(GROUP_F, part, recv_sem)
        matrix = top_matrix(tops, False)
        for side in range(2):
            unit, root = normalize(dot(matrix, set_ref[side, GROUP_BASE:top_base, cols]))
            top_unit_ref[side, :, cols] = unit
            top_root_ref[side, :, cols] = root
            set_ref[side, mine, cols] = unit.astype(jnp.bfloat16)
        for peer in grp_peers:
            block = set_ref.at[:, mine, cols]
            send(TOP_F, part, block, block, (peer, seq))

    def attend_part(part):
        cols = cols_of(part)
        wait(NEAR_F, part, recv_sem)
        wait(TOP_F, part, recv_sem)

        def one_pair(pair, carry):
            @pl.when(jnp.logical_and(pair == 1, part >= 1))
            def _():
                group_part(part - 1)

            lanes = pl.ds(pl.multiple_of(part * WIDTH + pair * PAIR, PAIR), PAIR)
            output, query_grad, row_grads, spans = attend_pair(
                lanes, live, query_ref, grad_ref, set_ref, score_ref, prob_ref, sgrad_ref
            )
            out_ref[:, lanes] = output
            query_grad_ref[:, lanes] = query_grad
            for start, stop in spans:
                both = row_grads(start, stop)
                for side in range(2):
                    rows = both[side]
                    if stop <= BLOCK:
                        diag_ref[side, start:stop, lanes] = rows
                    elif stop <= GROUP_BASE:
                        near_out[0, side, :, lanes] = rows[:NEAR].astype(jnp.bfloat16)
                        near_out[1, side, :, lanes] = rows[NEAR:].astype(jnp.bfloat16)
                    else:
                        cut = max(0, min(stop, top_base) - start)
                        if cut:
                            low = start - GROUP_BASE
                            group_sum_ref[side, low : low + cut, lanes] = rows[:cut]
                        if start + cut < stop:
                            low, high = start + cut - top_base, stop - top_base
                            top_out[side, low:high, lanes] = rows[cut:].astype(jnp.bfloat16)
            @pl.when(pair == WIDTH // PAIR - 1)
            def _():
                for slot, peer in enumerate(grp_peers):
                    block = top_out.at[:, rows_of(0, tops, peer), cols]
                    send(TOP_B, part, block, top_in.at[slot, :, :, cols], (peer, seq))

            for way, peer in enumerate((before_id, after_id)):
                source = near_out.at[way, :, :, lanes]
                send(NEAR_B, part, source, near_in.at[way, :, :, lanes], peer)
            return carry

        lax.fori_loop(0, WIDTH // PAIR, one_pair, 0)
    def group_part(part):
        cols = cols_of(part)
        wait(TOP_B, part, recv_sem)
        spread = top_matrix(tops, True)
        for side in range(2):
            upstream = top_out[side, rows_of(0, tops, grp), cols].astype(jnp.float32)
            for slot in range(grp_count - 1):
                upstream += top_in[slot, side, :, cols].astype(jnp.float32)
            back = pull_back(top_unit_ref[side, :, cols], top_root_ref[side, :, cols], upstream)
            group_out[side, :, cols] = (
                group_sum_ref[side, :, cols] + dot(spread, back.astype(jnp.bfloat16))
            ).astype(jnp.bfloat16)
        for slot, peer in enumerate(seq_peers):
            block = group_out.at[:, rows_of(0, OWN, peer), cols]
            send(GROUP_B, part, block, group_in.at[slot, :, :, cols], (grp, peer))

    def final_part(part):
        cols = cols_of(part)
        wait(NEAR_B, part, recv_sem)
        wait(GROUP_B, part, recv_sem)
        spread = pool_matrix(True)
        for side, result in enumerate((key_grad_ref, value_grad_ref)):
            near = near_in[0, side, :, cols].astype(jnp.float32)
            near += near_in[1, side, :, cols].astype(jnp.float32)
            group = group_out[side, rows_of(0, OWN, seq), cols].astype(jnp.float32)
            for slot in range(seq_count - 1):
                group += group_in[slot, side, :, cols].astype(jnp.float32)
            upstream = jnp.concatenate([near, group], axis=0)
            back = pull_back(unit_ref[side, :, cols], root_ref[side, :, cols], upstream)
            result[:, cols] = (
                diag_ref[side, :, cols] + dot(spread, back.astype(jnp.bfloat16))
            ).astype(jnp.bfloat16)

    lax.fori_loop(0, parts, summarize_part, 0)
    send_near(parts - 1)
    top_part(0)

    def stage(index, carry):
        @pl.when(index + 1 < parts)
        def _():
            top_part(index + 1)

        @pl.when(index < parts)
        def _():
            attend_part(index)

        @pl.when(index == parts)
        def _():
            group_part(index - 1)

        @pl.when(index >= 2)
        def _():
            final_part(index - 2)

        return carry

    lax.fori_loop(0, parts + 2, stage, 0)
    for part in range(parts):
        for kind in range(6):
            wait(kind, part, send_sem)


def store_kernel(*refs):
    for i in range(4):
        refs[i + 4][...] = refs[i][...]


def per_device(grp_count, seq_count, queries, keys, values, out_grad):
    rows, width = queries.shape
    group_rows = OWN * seq_count
    tops = 2 * seq_count
    count = GROUP_BASE + group_rows + tops * grp_count
    parts = width // WIDTH
    whole = pl.BlockSpec(memory_space=pltpu.VMEM)
    shape = jax.ShapeDtypeStruct((rows, width), jnp.bfloat16)
    low, high = jnp.bfloat16, jnp.float32
    results = pl.pallas_call(
        functools.partial(layer_kernel, grp_count, seq_count),
        out_shape=(shape,) * 4,
        in_specs=[whole] * 4,
        out_specs=(whole,) * 4,
        scratch_shapes=[
            pltpu.VMEM((2, count, width), low),
            pltpu.VMEM((2, NEAR, width), low),
            pltpu.VMEM((2, SUMS, width), high),
            pltpu.VMEM((2, SUMS, width), high),
            pltpu.VMEM((2, tops, width), high),
            pltpu.VMEM((2, tops, width), high),
            pltpu.VMEM((count, rows), high),
            pltpu.VMEM((2, count, rows), low),
            pltpu.VMEM((2, count, rows), low),
            pltpu.VMEM((2, rows, width), high),
            pltpu.VMEM((2, group_rows, width), high),
            pltpu.VMEM((2, 2, NEAR, width), low),
            pltpu.VMEM((2, 2, NEAR, width), low),
            pltpu.VMEM((2, group_rows, width), low),
            pltpu.VMEM((seq_count - 1, 2, OWN, width), low),
            pltpu.VMEM((2, tops * grp_count, width), low),
            pltpu.VMEM((grp_count - 1, 2, tops, width), low),
            pltpu.SemaphoreType.DMA((6, parts)),
            pltpu.SemaphoreType.DMA((6, parts)),
        ],
        compiler_params=pltpu.CompilerParams(
            vmem_limit_bytes=60 * 2**20, collective_id=0, has_side_effects=True
        ),
    )(queries, keys, values, out_grad)
    slab = pl.BlockSpec((rows // 4, width), lambda i: (i, 0))
    return pl.pallas_call(
        store_kernel,
        out_shape=(shape,) * 4,
        grid=(4,),
        in_specs=[slab] * 4,
        out_specs=(slab,) * 4,
        compiler_params=pltpu.CompilerParams(vmem_limit_bytes=60 * 2**20),
    )(*results)


def solution(mesh):
    spec = P(("grp", "seq"), None)
    return jax.shard_map(
        functools.partial(per_device, mesh.shape["grp"], mesh.shape["seq"]),
        mesh=mesh,
        in_specs=(spec,) * 4,
        out_specs=(spec,) * 4,
        check_vma=False,
    )
```
